32 devices in a mesh: groups: 2 (over x), ctx: 16 (over z, y, core).
Axes of the slice: x: 2, y: 2, z: 4, core: 2. Of those that a mesh axis runs over, the one named last changes fastest.
Arguments:
- queries: bfloat16 [8192, 2560], P(('groups', 'ctx')), parts along dimension 0, may hold values from -6 to 6
- keys: bfloat16 [8192, 2560], P(('groups', 'ctx')), parts along dimension 0, may hold values from -6 to 6
- values: bfloat16 [8192, 2560], P(('groups', 'ctx')), parts along dimension 0, may hold values from -6 to 6
- kv_lists: int32 [16, 4, 2, 8], P('ctx'), may hold values from 0 to 7, as said below
- kv_counts: int32 [16, 4, 2], P('ctx'), may hold values from 0 to 8, as said below
Outputs:
- attended: bfloat16 [8192, 2560], P(('groups', 'ctx')), parts along dimension 0
The draws below stay inside these ranges and needn't reach their ends.
There are 2 independent parts, one for each index of `groups`. The reference program is written for one: setup_inputs(seed, part) draws one part's arguments, and reference() takes and returns one part's arrays. A program takes and returns all parts, laid end to end along the dimension named above; an argument that names none is the same for every part. Nothing has to cross between parts.
Inputs may be any that keep to these rules, and one draw needn't show every extreme that they name: For every device d, level k and side s, the first 8 // 2**k entries of kv_lists[d, k, s] are distinct block indices; later entries are never read. kv_counts[d, k, s] is at most 8 // 2**k and reaches it for some device at every level and side; it is 0 exactly where the partner d - 2**k (s = 0) or d + 2**k (s = 1) lies outside 0 to 15, else 1 or more.
All inputs are finite; a program needn't handle non-finite values.
Results may differ from the reference program's by a relative error of at most 0.005.
Values may be sent and summed in bfloat16 or wider, within the bound.
No kernel may reach another device: no remote copies, remote signals or barrier semaphores. Data moves between devices by JAX's collectives and lax.ppermute only.
A program may use at most 128 MiB of HBM per device.

```python
import math
import jax
import jax.numpy as jnp
from jax import lax

HEADS = 20
HEAD = 128
ROWS = 256
NBLK = 8
LEVELS = 4
BS = 32
TOKENS = 4096
N_CTX = 16


def draw_queries(key, part):
    base_rows = jax.random.normal(jax.random.fold_in(key, 1), (TOKENS, HEADS * HEAD), jnp.float32) * 1.8
    return jnp.clip(base_rows, -6.0, 6.0).astype(jnp.bfloat16)


def draw_keys(key, part):
    base_rows = jax.random.normal(jax.random.fold_in(key, 2), (TOKENS, HEADS * HEAD), jnp.float32)
    return jnp.clip(base_rows, -6.0, 6.0).astype(jnp.bfloat16)


def draw_kv_lists(key, part):
    random_keys = jax.random.randint(jax.random.fold_in(key, 21), (N_CTX, LEVELS, 2, NBLK), 0, 1 << 20)
    random_keys = random_keys * NBLK + jnp.arange(NBLK, dtype=jnp.int32)
    return jnp.argsort(random_keys, axis=-1).astype(jnp.int32)


def draw_kv_counts(key, part):
    device_ids = jnp.arange(N_CTX, dtype=jnp.int32)[:, None, None]
    level_ids = jnp.arange(LEVELS, dtype=jnp.int32)[None, :, None]
    side_ids = jnp.arange(2, dtype=jnp.int32)[None, None, :]
    distance = jnp.left_shift(jnp.int32(1), level_ids)
    partner = jnp.where(side_ids == 0, device_ids - distance, device_ids + distance)
    present = (partner >= 0) & (partner < N_CTX)
    capacity = NBLK // distance
    random_pick = jax.random.randint(jax.random.fold_in(key, 22), (N_CTX, LEVELS, 2), 0, 1 << 20) % capacity + 1
    saturated = device_ids % 4 == 0
    counted = jnp.where(present, jnp.where(saturated, capacity, random_pick), 0)
    return counted.astype(jnp.int32)


def shard_levels(rng, shape, shards, low, top_value):
    def one(position, parts):
        steps = jax.random.uniform(jax.random.fold_in(jax.random.fold_in(rng, 6), position), (parts,), jnp.float32, low / len(shards), top_value / len(shards))
        return jnp.repeat(jnp.exp(steps), shape[position] // parts).reshape((-1,) + (1,) * (len(shape) - position - 1))

    level = one(*shards[0])
    for cut in shards[1:]:
        level = level * one(*cut)
    return level


def noise(own_key, extent, deviation, limit, split=(), kind=jnp.bfloat16):
    values = deviation * jax.random.normal(own_key, extent, jnp.float32)
    if split:
        values = values * shard_levels(own_key, extent, split, -0.22, 0.18)
    return jnp.clip(values, -limit, limit).astype(kind)


def setup_inputs(seed: int = 0, part: int = 0) -> dict:
    streams_of = jax.random.split(jax.random.key(seed), 6)
    part_splits = jax.random.split(jax.random.fold_in(streams_of[5], part), 6)
    return {
        "queries": draw_queries(jax.random.fold_in(jax.random.fold_in(streams_of[5], part), 71), part),
        "keys": draw_keys(jax.random.fold_in(jax.random.fold_in(streams_of[5], part), 71), part),
        "values": noise(part_splits[2], (TOKENS, HEADS * HEAD), 1.0, 6.0, ((0, 16),)),
        "kv_lists": draw_kv_lists(jax.random.fold_in(streams_of[5], 71), part),
        "kv_counts": draw_kv_counts(jax.random.fold_in(streams_of[5], 71), part),
    }


def reference(queries, keys, values, kv_lists, kv_counts):
    width = HEADS * HEAD
    key_blocks = keys.reshape(N_CTX, NBLK, BS, width)
    value_blocks = values.reshape(N_CTX, NBLK, BS, width)

    def one_device(device_id):
        query_rows = lax.dynamic_slice_in_dim(queries, device_id * ROWS, ROWS, 0)
        key_parts = [key_blocks[device_id].reshape(ROWS, width)]
        value_parts = [value_blocks[device_id].reshape(ROWS, width)]
        flag_parts = [jnp.ones((ROWS,), dtype=bool)]
        for level_id in range(LEVELS):
            distance = 2 ** level_id
            capacity = NBLK // distance
            for side_id in range(2):
                partner = device_id - distance if side_id == 0 else device_id + distance
                safe_partner = jnp.clip(partner, 0, N_CTX - 1).astype(jnp.int32)
                chosen = kv_lists[device_id, level_id, side_id, :capacity].astype(jnp.int32)
                counted = kv_counts[device_id, level_id, side_id]
                key_parts.append(key_blocks[safe_partner][chosen].reshape(capacity * BS, width))
                value_parts.append(value_blocks[safe_partner][chosen].reshape(capacity * BS, width))
                slot_ids = jnp.arange(capacity * BS, dtype=jnp.int32) // BS
                flag_parts.append(slot_ids < counted)
        all_keys = jnp.concatenate(key_parts, axis=0).astype(jnp.float32)
        all_values = jnp.concatenate(value_parts, axis=0).astype(jnp.float32)
        allowed = jnp.concatenate(flag_parts, axis=0)
        query_heads = query_rows.astype(jnp.float32).reshape(ROWS, HEADS, HEAD)
        key_heads = all_keys.reshape(-1, HEADS, HEAD)
        value_heads = all_values.reshape(-1, HEADS, HEAD)
        scores = jnp.einsum('qhd,khd->hqk', query_heads, key_heads) * (1.0 / math.sqrt(HEAD))
        scores = jnp.where(allowed[None, None, :], scores, -1e+30)
        top_score = lax.optimization_barrier(jnp.max(scores, axis=-1, keepdims=True))
        weights = jnp.exp(scores - top_score)
        weight_total = lax.optimization_barrier(jnp.sum(weights, axis=-1))
        rounded = lax.optimization_barrier(weights.astype(jnp.bfloat16)).astype(jnp.float32)
        mixed_values = jnp.einsum('hqk,khd->qhd', rounded, value_heads)
        result = mixed_values / jnp.transpose(weight_total)[:, :, None]
        return result.reshape(ROWS, width).astype(jnp.bfloat16)
    results = lax.map(one_device, jnp.arange(N_CTX, dtype=jnp.int32))
    return results.reshape(TOKENS, width)
```

```python
import functools
import math

import jax
import jax.numpy as jnp
from jax import lax
from jax.experimental import pallas as pl
from jax.experimental.pallas import tpu as pltpu
from jax.sharding import PartitionSpec as P

HEAD = 128
UNROLL = 20
MASKED = -1e30
F32 = jnp.float32
BF16 = jnp.bfloat16
VMEM = 16 * 1024 * 1024
COST = pl.CostEstimate(flops=1000, bytes_accessed=1000, transcendentals=0)


def permute(block, count, route):
    pairs = [(a, b) for a, b in route if 0 <= a < count and 0 <= b < count]
    return lax.ppermute(block, "ctx", pairs)


def listed(lists, device, level, side, j, shape):
    device = jnp.clip(device, 0, shape["devices"] - 1)
    return lists[device, (level * 2 + side) * shape["blocks"] + j]


def others(found, lists, device, side, shape):
    blocks = shape["blocks"]
    half = blocks // 2
    names = [listed(lists, device, 1, side, j, shape) for j in range(half)]
    place = jnp.int32(0)
    for b in range(blocks):
        named = functools.reduce(jnp.logical_or, [n == b for n in names])
        found[place] = jnp.int32(b)
        place = place + jnp.where(named, 0, 1)


def rows_at(ref, block, rows):
    return ref.at[pl.ds(pl.multiple_of(block * rows, rows), rows)]


class Copies:
    def __init__(self, sems):
        self.sems = sems
        self.started = []

    def start(self, source, target):
        copy = pltpu.make_async_copy(source, target, self.sems.at[len(self.started)])
        copy.start()
        self.started.append(copy)

    def wait(self):
        for copy in self.started:
            copy.wait()


def first_pack(shape, lists, keys, values, second, along, *rest):
    far = rest[: -2]
    found, sems = rest[-2:]
    rows = shape["rows"]
    half = shape["blocks"] // 2
    me = lax.axis_index("ctx")
    spot = me % 4
    outer = jnp.logical_or(spot == 0, spot == 3)

    def gather(copies, target, names):
        n = len(names)
        for j, name in enumerate(names):
            copies.start(rows_at(keys, name, rows), target.at[pl.ds(j * rows, rows)])
            copies.start(rows_at(values, name, rows), target.at[pl.ds((n + j) * rows, rows)])

    reader = jnp.where(spot == 0, me + 2, me - 2)
    side = jnp.where(spot == 0, 0, 1)
    others(found, lists, reader, side, shape)
    copies = Copies(sems)
    at = 0
    for level in range(2, shape["levels"]):
        for way in range(2):
            device = me + (1 << level) * (1 - 2 * way)
            capacity = shape["blocks"] >> level
            gather(copies, far[at], [listed(lists, device, level, way, j, shape) for j in range(capacity)])
            at += 1

    @pl.when(outer)
    def _():
        more = Copies(sems.at[pl.ds(len(copies.started), 4 * half)])
        gather(more, along, [found[j] for j in range(half)])
        gather(more, second, [listed(lists, reader, 1, side, j, shape) for j in range(half)])
        more.wait()

    @pl.when(jnp.logical_not(outer))
    def _():
        copy = pltpu.make_async_copy(values, second, sems.at[len(copies.started)])
        copy.start()
        copy.wait()

    copies.wait()


def second_pack(shape, lists, keys, values, along, across, third, sems):
    rows = shape["rows"]
    half = shape["blocks"] // 2
    me = lax.axis_index("ctx")
    spot = me % 4
    outer = jnp.logical_or(spot == 0, spot == 3)

    @pl.when(outer)
    def _():
        copies = Copies(sems)
        copies.start(values, across)
        copies.start(along, third)
        copies.wait()

    @pl.when(jnp.logical_not(outer))
    def _():
        copies = Copies(sems)
        near = jnp.where(spot == 1, me - 1, me + 1)
        far = jnp.where(spot == 1, me + 3, me - 3)
        near_side = jnp.where(spot == 1, 1, 0)
        far_side = jnp.where(spot == 1, 0, 1)
        for target, device, side in ((third, far, far_side), (across, near, near_side)):
            for j in range(half):
                name = listed(lists, device, 1, side, j, shape)
                copies.start(rows_at(keys, name, rows), target.at[pl.ds(j * rows, rows)])
                copies.start(rows_at(values, name, rows), target.at[pl.ds((half + j) * rows, rows)])
        copies.wait()


def pack_call(body, shape, lists, arrays, out_rows, scratch, copies):
    width = shape["width"]
    outs = tuple(jax.ShapeDtypeStruct((r, width), BF16) for r in out_rows)
    return pl.pallas_call(
        functools.partial(body, shape),
        out_shape=outs,
        in_specs=[pl.BlockSpec(memory_space=pltpu.SMEM)] + [pl.BlockSpec(memory_space=pltpu.HBM)] * len(arrays),
        out_specs=tuple([pl.BlockSpec(memory_space=pltpu.VMEM)] * len(outs)),
        scratch_shapes=scratch + [pltpu.SemaphoreType.DMA((copies,))],
        cost_estimate=COST,
        compiler_params=pltpu.CompilerParams(vmem_limit_bytes=VMEM),
    )(lists, *arrays)


def lanes(column, n):
    wide = jnp.concatenate([column] * -(-n // column.shape[1]), axis=1)
    return wide[:, :n]


def attend(query, state, keys, values, masks):
    scale = math.log2(math.e) / math.sqrt(HEAD)
    raw = lax.dot_general(query, keys, (((1,), (1,)), ((), ())), preferred_element_type=F32)
    scores = []
    at = 0
    for n, mask in masks:
        part = raw[:, at : at + n] * scale
        scores.append(part if mask is None else part + mask)
        at += n
    scores = scores[0] if len(scores) == 1 else jnp.concatenate(scores, axis=1)
    best = jnp.broadcast_to(jnp.max(scores, axis=1, keepdims=True), query.shape)
    if state is not None:
        best = jnp.maximum(best, state[0])
    weights = jnp.exp2(scores - lanes(best, scores.shape[1])).astype(BF16)
    both = jnp.dot(weights, jnp.concatenate([values, jnp.ones_like(values)], axis=1), preferred_element_type=F32)
    weighted, total = both[:, :HEAD], both[:, HEAD:]
    if state is not None:
        factor = jnp.exp2(state[0] - best)
        total = total + state[1] * factor
        weighted = weighted + state[2] * factor
    return best, total, weighted


def member_flags(flags, at, ids, lists, counts, me, level, side, shape):
    counted = counts[0, level, side]
    names = [listed(lists, me, level, side, j, shape) for j in range(shape["blocks"] >> level)]
    for n, b in enumerate(ids):
        seen = functools.reduce(
            jnp.logical_or, [jnp.logical_and(j < counted, name == b) for j, name in enumerate(names)]
        )
        flags[at + n] = jnp.where(seen, 0.0, MASKED).astype(F32)


def order_flags(flags, at, capacity, counts, level, side):
    counted = counts[0, level, side]
    for j in range(capacity):
        flags[at + j] = jnp.where(j < counted, 0.0, MASKED).astype(F32)


def spread(flags, at, count, rows):
    place = lax.broadcasted_iota(jnp.int32, (1, count * rows), 1)
    row = jnp.full((1, count * rows), flags[at], F32)
    for b in range(1, count):
        row = jnp.where(place >= b * rows, flags[at + b], row)
    return row


def over_heads(width, body):
    def step(h, _):
        body(pl.ds(pl.multiple_of(h * HEAD, HEAD), HEAD))
        return 0

    lax.fori_loop(0, width // HEAD, step, 0, unroll=math.gcd(UNROLL, width // HEAD))


def load_state(refs, c):
    return tuple(ref[:, c] for ref in refs)


def store_state(refs, c, state):
    for ref, part in zip(refs, state):
        ref[:, c] = part


def near_kernel(shape, lists, counts, q, k, v, ak, av, best, total, weighted, flags):
    me = lax.axis_index("ctx")
    blocks = shape["blocks"]
    member_flags(flags, 0, range(blocks), lists, counts, me, 0, 1 - me % 2, shape)
    mask = spread(flags, 0, blocks, shape["rows"])

    def head(c):
        keys = jnp.concatenate([k[:, c], ak[:, c]], axis=0)
        values = jnp.concatenate([v[:, c], av[:, c]], axis=0)
        state = attend(q[:, c], None, keys, values, [(k.shape[0], None), (ak.shape[0], mask)])
        store_state((best, total, weighted), c, state)

    over_heads(shape["width"], head)


def packed(refs, c, filler=0):
    keys = [ref[: ref.shape[0] // 2, c] for ref in refs]
    values = [ref[ref.shape[0] // 2 :, c] for ref in refs]
    if filler:
        keys.append(jnp.zeros((filler, HEAD), BF16))
        values.append(jnp.zeros((filler, HEAD), BF16))
    return jnp.concatenate(keys, axis=0), jnp.concatenate(values, axis=0)


def listed_kernel(shape, sides, lists, counts, q, *refs):
    n = len(sides)
    sources, before, after, flags = refs[:n], refs[n : n + 3], refs[n + 3 : n + 6], refs[-1]
    me = lax.axis_index("ctx")
    at = 0
    for level, side in sides:
        capacity = shape["blocks"] >> level
        order_flags(flags, at, capacity, counts, level, side(me))
        at += capacity
    rows = shape["rows"]
    filler = -at % shape["blocks"]
    for b in range(filler):
        flags[at + b] = jnp.float32(MASKED)
    mask = spread(flags, 0, at + filler, rows)

    def head(c):
        keys, values = packed(sources, c, filler * rows)
        store_state(after, c, attend(q[:, c], load_state(before, c), keys, values, [(keys.shape[0], mask)]))

    over_heads(shape["width"], head)


def giver_ids(found, lists, device, side, shape):
    half = shape["blocks"] // 2
    others(found, lists, device, side, shape)
    return [listed(lists, device, 1, side, j, shape) for j in range(half)] + [found[j] for j in range(half)]


def full_kernel(shape, lists, counts, q, zeroth, second, third, fourth, *refs):
    before, after, flags, found = refs[:3], refs[3:6], refs[6], refs[7]
    me = lax.axis_index("ctx")
    spot = me % 4
    blocks = shape["blocks"]
    outer = jnp.logical_or(spot == 0, spot == 3)
    ids = giver_ids(found, lists, jnp.where(spot == 0, me - 3, me + 3), jnp.where(spot == 0, 1, 0), shape)
    ids = [jnp.where(outer, name, b) for b, name in enumerate(ids)]
    member_flags(flags, 0, ids, lists, counts, me, 0, me % 2, shape)

    def head(c, keys, values):
        mask = spread(flags, 0, blocks, shape["rows"])
        store_state(after, c, attend(q[:, c], load_state(before, c), keys, values, [(keys.shape[0], mask)]))

    @pl.when(outer)
    def _():
        over_heads(shape["width"], lambda c: head(c, *packed([fourth, third], c)))

    @pl.when(jnp.logical_not(outer))
    def _():
        over_heads(shape["width"], lambda c: head(c, zeroth[:, c], second[:, c]))


def last_kernel(shape, lists, counts, q, fourth, third, *refs):
    before, out, flags, found = refs[:3], refs[3], refs[4], refs[5]
    me = lax.axis_index("ctx")
    spot = me % 4
    blocks = shape["blocks"]
    half = blocks // 2
    outer = jnp.logical_or(spot == 0, spot == 3)
    side = jnp.where(spot < 2, 0, 1)

    @pl.when(outer)
    def _():
        for j in range(half):
            flags[j] = jnp.float32(MASKED)
        order_flags(flags, half, half, counts, 1, side)

    @pl.when(jnp.logical_not(outer))
    def _():
        ids = giver_ids(found, lists, jnp.where(spot == 1, me - 4, me + 4), jnp.where(spot == 1, 1, 0), shape)
        member_flags(flags, 0, ids, lists, counts, me, 1, side, shape)

    mask = spread(flags, 0, blocks, shape["rows"])

    def head(c):
        keys, values = packed([fourth, third], c)
        _, total, weighted = attend(q[:, c], load_state(before, c), keys, values, [(keys.shape[0], mask)])
        out[:, c] = (weighted / total).astype(BF16)

    over_heads(shape["width"], head)


def attend_call(body, shape, lists, counts, arrays, state, last, scratch, blocks_seen):
    queries, width = arrays[0].shape
    smem = pl.BlockSpec(memory_space=pltpu.SMEM)
    vmem = pl.BlockSpec(memory_space=pltpu.VMEM)
    return pl.pallas_call(
        functools.partial(body, shape),
        out_shape=jax.ShapeDtypeStruct((queries, width), BF16)
        if last
        else tuple([jax.ShapeDtypeStruct((queries, width), F32)] * 3),
        in_specs=[smem, smem] + [vmem] * (len(arrays) + len(state)),
        out_specs=vmem if last else tuple([vmem] * 3),
        scratch_shapes=[pltpu.SMEM((shape["blocks"] * 4,), F32)] + scratch,
        cost_estimate=COST,
        compiler_params=pltpu.CompilerParams(vmem_limit_bytes=VMEM),
    )(lists, counts, *arrays, *state)


def shards(queries, keys, values, kv_lists, kv_counts):
    row_count, width = queries.shape
    blocks = kv_lists.shape[3]
    levels = kv_lists.shape[1]
    devices = lax.axis_size("ctx")
    half = blocks // 2
    rows = row_count // blocks
    shape = {
        "devices": devices,
        "blocks": blocks,
        "levels": levels,
        "rows": rows,
        "width": width,
    }
    every = range(devices)
    spot = {i: [d for d in every if d % 4 == i] for i in range(4)}
    other_core = [(d, d ^ 1) for d in every]
    inner_swap = [(d, d ^ 3) for d in spot[1] + spot[2]]
    outer_swap = [(d, d ^ 3) for d in spot[0] + spot[3]]
    outer_along = [(d, d + 4) for d in spot[3]] + [(d, d - 4) for d in spot[0]]
    outer_on = [(d, d + 4) for d in spot[0]] + [(d, d - 4) for d in spot[3]]
    outer_in = [(d, d ^ 1) for d in spot[0] + spot[3]]
    inner_on = [(d, d + 4) for d in spot[1]] + [(d, d - 4) for d in spot[2]]

    zeroth = permute(keys, devices, inner_swap)
    sent = jnp.broadcast_to(kv_lists.reshape(1, -1), (devices, levels * 2 * blocks))
    lists = lax.all_to_all(sent, "ctx", 0, 0, tiled=True)

    far_levels = [(level, way) for level in range(2, levels) for way in range(2)]
    far_rows = [2 * (blocks >> level) * rows for level, _ in far_levels]
    packs = pack_call(
        first_pack,
        shape,
        lists,
        (keys, values),
        [row_count, row_count] + far_rows,
        [pltpu.SMEM((blocks + 1,), jnp.int32)],
        4 * half + sum(2 * (blocks >> level) for level, _ in far_levels),
    )
    along = permute(packs[1], devices, outer_along)
    second = permute(packs[0], devices, inner_swap + outer_swap)
    far = []
    for (level, way), pack in zip(far_levels, packs[2:]):
        step = (1 << level) * (1 - 2 * way)
        far.append(permute(pack, devices, [(d, d + step) for d in every]))
    other_keys = permute(keys, devices, other_core)
    other_values = permute(values, devices, other_core)

    state = attend_call(
        near_kernel, shape, lists, kv_counts, (queries, keys, values, other_keys, other_values), (), False, [], 2 * blocks
    )

    fourth = permute(second, devices, outer_on)
    across, third_out = pack_call(
        second_pack, shape, lists, (zeroth, second, along), [row_count, row_count], [], 4 * half
    )
    third = permute(third_out, devices, inner_on + outer_swap)
    middle = permute(across, devices, other_core)

    sides = [(1, lambda me: jnp.where(me % 4 < 2, 1, 0))]
    sides += [(level, lambda me, way=way: way) for level, way in far_levels]
    state = attend_call(
        functools.partial(rename, listed_kernel, sides),
        shape,
        lists,
        kv_counts,
        (queries, middle, *far),
        state,
        False,
        [],
        half + sum(blocks >> level for level, _ in far_levels),
    )
    handed = permute(third, devices, other_core)
    handed_fourth = permute(fourth, devices, outer_in)
    state = attend_call(
        full_kernel,
        shape,
        lists,
        kv_counts,
        (queries, zeroth, second, third, fourth),
        state,
        False,
        [pltpu.SMEM((blocks + 1,), jnp.int32)],
        blocks,
    )
    return attend_call(
        last_kernel,
        shape,
        lists,
        kv_counts,
        (queries, handed_fourth, handed),
        state,
        True,
        [pltpu.SMEM((blocks + 1,), jnp.int32)],
        blocks,
    )


def rename(body, sides, shape, *refs):
    return body(shape, sides, *refs)


def solution(mesh):
    in_specs = (
        P(("groups", "ctx"), None),
        P(("groups", "ctx"), None),
        P(("groups", "ctx"), None),
        P("ctx", None, None, None),
        P("ctx", None, None),
    )
    out_specs = P(("groups", "ctx"), None)
    return jax.shard_map(shards, mesh=mesh, in_specs=in_specs, out_specs=out_specs, check_vma=False)
```

```python
import functools
import math

import jax
import jax.numpy as jnp
from jax import lax
from jax.experimental import pallas as pl
from jax.experimental.pallas import tpu as pltpu
from jax.sharding import PartitionSpec as P

HEAD = 128
UNROLL = 20
MASKED = -1e30
F32 = jnp.float32
BF16 = jnp.bfloat16
VMEM = 8 * 1024 * 1024
COST = pl.CostEstimate(flops=1000, bytes_accessed=1000, transcendentals=0)


def permute(block, count, route):
    pairs = [(a, b) for a, b in route if 0 <= a < count and 0 <= b < count]
    return lax.ppermute(block, "ctx", pairs)


def listed(lists, device, level, side, j, shape):
    device = jnp.clip(device, 0, shape["devices"] - 1)
    return lists[device, (level * 2 + side) * shape["blocks"] + j]


def others(found, names, blocks):
    place = jnp.int32(0)
    for b in range(blocks):
        named = functools.reduce(jnp.logical_or, [n == b for n in names])
        found[place] = jnp.int32(b)
        place = place + jnp.where(named, 0, 1)


def gather(source, target, names, rows, at=0):
    below = source.shape[0] // 2
    for shift in (0, below):
        for name in names:
            target[at : at + rows] = source[pl.ds(pl.multiple_of(name * rows + shift, rows), rows)]
            at += rows
    return at


def far_pack(shape, lists, own, *far):
    me = lax.axis_index("ctx")
    for (level, way), out in zip(shape["far"], far):
        device = me + (1 << level) * (1 - 2 * way)
        names = [listed(lists, device, level, way, j, shape) for j in range(shape["blocks"] >> level)]
        gather(own, out, names, shape["rows"])


def crossing_names(found, lists, me, inner, shape):
    first = inner % 4 == 1
    half = shape["blocks"] // 2
    reader = jnp.where(first, inner - 2, inner + 2)
    names = [listed(lists, reader, 1, jnp.where(first, 1, 0), j, shape) for j in range(half)]
    others(found, names, shape["blocks"])
    return names, [found[j] for j in range(half)]


def reader_names(lists, me, shape):
    first = me % 4 == 0
    reader = jnp.where(first, me + 2, me - 2)
    return [listed(lists, reader, 1, jnp.where(first, 0, 1), j, shape) for j in range(shape["blocks"] // 2)]


def first_pack(shape, lists, own, crossing, *refs):
    far, found = refs[:-1], refs[-1]
    far_pack(shape, lists, own, *far)
    half = shape["blocks"] // 2
    me = lax.axis_index("ctx")
    spot = me % 4
    outer = jnp.logical_or(spot == 0, spot == 3)

    @pl.when(outer)
    def _():
        gather(own, crossing, reader_names(lists, me, shape), shape["rows"])

    @pl.when(jnp.logical_not(outer))
    def _():
        names, _ = crossing_names(found, lists, me, me, shape)
        gather(own, crossing, names, shape["rows"])


def second_pack(shape, lists, own, other, out, along, found):
    me = lax.axis_index("ctx")
    spot = me % 4
    outer = jnp.logical_or(spot == 0, spot == 3)
    quarter = shape["blocks"] // 4

    @pl.when(outer)
    def _():
        _, rest = crossing_names(found, lists, me, jnp.where(spot == 0, me + 1, me - 1), shape)
        gather(other, out, rest[quarter:], shape["rows"])
        others(found, reader_names(lists, me, shape), shape["blocks"])
        gather(own, along, [found[j] for j in range(2 * quarter)], shape["rows"])

    @pl.when(jnp.logical_not(outer))
    def _():
        _, rest = crossing_names(found, lists, me, me, shape)
        gather(own, out, rest[:quarter], shape["rows"])


SMEM = pl.BlockSpec(memory_space=pltpu.SMEM)
IN_VMEM = pl.BlockSpec(memory_space=pltpu.VMEM)


def pack_call(body, shape, lists, arrays, out_rows, scratch=()):
    width = arrays[0].shape[1]
    return pl.pallas_call(
        functools.partial(body, shape),
        out_shape=tuple(jax.ShapeDtypeStruct((r, width), BF16) for r in out_rows),
        in_specs=[SMEM] + [IN_VMEM] * len(arrays),
        out_specs=tuple([IN_VMEM] * len(out_rows)),
        scratch_shapes=list(scratch),
        cost_estimate=COST,
        compiler_params=pltpu.CompilerParams(vmem_limit_bytes=VMEM),
    )(lists, *arrays)


def lanes(column, n):
    wide = jnp.concatenate([column] * -(-n // column.shape[1]), axis=1)
    return wide[:, :n]


def attend(query, state, keys, values, masks):
    scale = math.log2(math.e) / math.sqrt(HEAD)
    raw = lax.dot_general(query, keys, (((1,), (1,)), ((), ())), preferred_element_type=F32)
    scores = []
    at = 0
    for n, mask in masks:
        part = raw[:, at : at + n] * scale
        scores.append(part if mask is None else part + mask)
        at += n
    scores = scores[0] if len(scores) == 1 else jnp.concatenate(scores, axis=1)
    best = jnp.broadcast_to(jnp.max(scores, axis=1, keepdims=True), query.shape)
    if state is not None:
        best = jnp.maximum(best, state[0])
    weights = jnp.exp2(scores - lanes(best, scores.shape[1])).astype(BF16)
    both = jnp.dot(weights, jnp.concatenate([values, jnp.ones_like(values)], axis=1), preferred_element_type=F32)
    weighted, total = both[:, :HEAD], both[:, HEAD:]
    if state is not None:
        factor = jnp.exp2(state[0] - best)
        total = total + state[1] * factor
        weighted = weighted + state[2] * factor
    return best, total, weighted


def member_flags(flags, at, ids, lists, counts, me, level, side, shape):
    counted = counts[0, level, side]
    names = [listed(lists, me, level, side, j, shape) for j in range(shape["blocks"] >> level)]
    for n, b in enumerate(ids):
        seen = functools.reduce(
            jnp.logical_or, [jnp.logical_and(j < counted, name == b) for j, name in enumerate(names)]
        )
        flags[at + n] = jnp.where(seen, 0.0, MASKED).astype(F32)


def order_flags(flags, at, capacity, counts, level, side):
    counted = counts[0, level, side]
    for j in range(capacity):
        flags[at + j] = jnp.where(j < counted, 0.0, MASKED).astype(F32)


def spread(flags, at, count, rows):
    place = lax.broadcasted_iota(jnp.int32, (1, count * rows), 1)
    row = jnp.full((1, count * rows), flags[at], F32)
    for b in range(1, count):
        row = jnp.where(place >= b * rows, flags[at + b], row)
    return row


def over_heads(width, body):
    def step(h, _):
        body(pl.ds(pl.multiple_of(h * HEAD, HEAD), HEAD))
        return 0

    lax.fori_loop(0, width // HEAD, step, 0, unroll=math.gcd(UNROLL, width // HEAD))


def load_state(refs, c):
    return tuple(ref[:, c] for ref in refs)


def store_state(refs, c, state):
    for ref, part in zip(refs, state):
        ref[:, c] = part


def far_sources(parts, refs, flags, at, counts, shape):
    sources = []
    for number, level, side in parts:
        capacity = shape["blocks"] >> level
        order_flags(flags, at, capacity, counts, level, side)
        sources.append((refs[number], 0, 2 * capacity * shape["rows"]))
        at += capacity
    return sources, at


def near_kernel(shape, lists, counts, q, own, other, *refs):
    after, flags = refs[-4:-1], refs[-1]
    me = lax.axis_index("ctx")
    blocks = shape["blocks"]
    member_flags(flags, 0, range(blocks), lists, counts, me, 0, 1 - me % 2, shape)
    mask = spread(flags, 0, blocks, shape["rows"])

    def head(c):
        keys, values = packed([own, other], c)
        masks = [(own.shape[0] // 2, None), (other.shape[0] // 2, mask)]
        store_state(after, c, attend(q[:, c], None, keys, values, masks))

    over_heads(shape["width"], head)


def packed(refs, c, filler=0):
    keys, values = [], []
    for ref in refs:
        ref, at, count = ref if isinstance(ref, tuple) else (ref, 0, ref.shape[0])
        keys.append(ref[at : at + count // 2, c])
        values.append(ref[at + count // 2 : at + count, c])
    if filler:
        keys.append(jnp.zeros((filler, HEAD), BF16))
        values.append(jnp.zeros((filler, HEAD), BF16))
    return jnp.concatenate(keys, axis=0), jnp.concatenate(values, axis=0)


def more_heads(shape, flags, count, q, before, after, sources):
    filler = -count % shape["blocks"]
    for b in range(count, count + filler):
        flags[b] = jnp.float32(MASKED)
    mask = spread(flags, 0, count + filler, shape["rows"])

    def head(c):
        keys, values = packed(sources, c, filler * shape["rows"])
        store_state(after, c, attend(q[:, c], load_state(before, c), keys, values, [(keys.shape[0], mask)]))

    over_heads(shape["width"], head)


def quad_kernel(shape, lists, counts, q, crossed, crossed_core, *refs):
    far, before, after, flags, found = refs[:-8], refs[-8:-5], refs[-5:-2], refs[-2], refs[-1]
    me = lax.axis_index("ctx")
    spot = me % 4
    blocks = shape["blocks"]
    half = blocks // 2
    begun = 0
    for level, way in shape["far"]:
        order_flags(flags, begun, blocks >> level, counts, level, way)
        begun += blocks >> level
    near_side = jnp.where(spot < 2, 1, 0)
    outer = jnp.logical_or(spot == 0, spot == 3)

    @pl.when(outer)
    def _():
        names, _ = crossing_names(found, lists, me, jnp.where(spot == 0, me + 2, me - 2), shape)
        member_flags(flags, begun, names, lists, counts, me, 1, near_side, shape)
        more_heads(shape, flags, begun + half, q, before, after, [*far, crossed])

    @pl.when(jnp.logical_not(outer))
    def _():
        order_flags(flags, begun, half, counts, 1, near_side)
        names, _ = crossing_names(found, lists, me, jnp.where(spot == 1, me + 1, me - 1), shape)
        member_flags(flags, begun + half, names, lists, counts, me, 0, me % 2, shape)
        more_heads(shape, flags, begun + 2 * half, q, before, after, [*far, crossed, crossed_core])


def giver_names(found, lists, me, shape):
    spot = me % 4
    outer = jnp.logical_or(spot == 0, spot == 3)
    step = jnp.where(outer, 3, 4)
    giver = jnp.where(spot < 2, me - step, me + step)
    half = shape["blocks"] // 2
    names = [listed(lists, giver, 1, jnp.where(spot < 2, 1, 0), j, shape) for j in range(half)]
    others(found, names, shape["blocks"])
    return names, [found[j] for j in range(half)]


def passed_kernel(shape, lists, counts, q, rest, rest_core, passed, *refs):
    before, after, flags, found = refs[:3], refs[3:6], refs[6], refs[7]
    me = lax.axis_index("ctx")
    spot = me % 4
    blocks = shape["blocks"]
    half = blocks // 2
    quarter = blocks // 4
    outer = jnp.logical_or(spot == 0, spot == 3)
    far_side = jnp.where(spot < 2, 0, 1)

    @pl.when(outer)
    def _():
        _, others_ = crossing_names(found, lists, me, jnp.where(spot == 0, me + 2, me - 2), shape)
        member_flags(flags, 0, others_, lists, counts, me, 1, jnp.where(spot < 2, 1, 0), shape)
        order_flags(flags, half, half, counts, 1, far_side)

    @pl.when(jnp.logical_not(outer))
    def _():
        _, others_ = crossing_names(found, lists, me, jnp.where(spot == 1, me + 1, me - 1), shape)
        member_flags(flags, 0, others_[quarter:] + others_[:quarter], lists, counts, me, 0, me % 2, shape)
        names, _ = giver_names(found, lists, me, shape)
        member_flags(flags, half, names, lists, counts, me, 1, far_side, shape)

    more_heads(shape, flags, 2 * half, q, before, after, [rest, rest_core, passed])


def last_kernel(shape, lists, counts, q, passed_core, third, third_core, *refs):
    before, out, flags, found = refs[:3], refs[3], refs[4], refs[5]
    me = lax.axis_index("ctx")
    spot = me % 4
    blocks = shape["blocks"]
    half = blocks // 2
    names, rest = giver_names(found, lists, me, shape)
    outer = jnp.logical_or(spot == 0, spot == 3)

    def heads(sources):
        mask = spread(flags, 0, blocks, shape["rows"])

        def head(c):
            keys, values = packed(sources, c, (blocks - half * len(sources)) * shape["rows"])
            _, total, weighted = attend(q[:, c], load_state(before, c), keys, values, [(keys.shape[0], mask)])
            out[:, c] = (weighted / total).astype(BF16)

        over_heads(shape["width"], head)

    @pl.when(outer)
    def _():
        member_flags(flags, 0, names + rest, lists, counts, me, 0, me % 2, shape)
        heads([passed_core, third])

    @pl.when(jnp.logical_not(outer))
    def _():
        member_flags(flags, 0, rest, lists, counts, me, 1, jnp.where(spot < 2, 0, 1), shape)
        for b in range(half, blocks):
            flags[b] = jnp.float32(MASKED)
        heads([third_core])


def attend_call(body, shape, smem, arrays, state=(), last=False, scratch=()):
    queries, width = arrays[0].shape
    return pl.pallas_call(
        functools.partial(body, shape),
        out_shape=jax.ShapeDtypeStruct((queries, width), BF16)
        if last
        else tuple([jax.ShapeDtypeStruct((queries, width), F32)] * 3),
        in_specs=[SMEM] * len(smem) + [IN_VMEM] * (len(arrays) + len(state)),
        out_specs=IN_VMEM if last else tuple([IN_VMEM] * 3),
        scratch_shapes=[pltpu.SMEM((64,), F32), *scratch],
        cost_estimate=COST,
        compiler_params=pltpu.CompilerParams(vmem_limit_bytes=VMEM),
    )(*smem, *arrays, *state)


def after(value, *events):
    return lax.optimization_barrier((value, *events))[0]


def shards(queries, keys, values, kv_lists, kv_counts):
    row_count, width = queries.shape
    blocks = kv_lists.shape[3]
    levels = kv_lists.shape[1]
    devices = lax.axis_size("ctx")
    half = blocks // 2
    rows = row_count // blocks
    shape = {"devices": devices, "blocks": blocks, "rows": rows, "width": width, "far": [(level, way) for level in range(2, levels) for way in range(2)]}
    every = range(devices)
    spot = {i: [d for d in every if d % 4 == i] for i in range(4)}
    other_core = [(d, d ^ 1) for d in every]
    over_y = [(d, d ^ 2) for d in every]
    outer_swap = [(d, d ^ 3) for d in spot[0] + spot[3]]
    outer_along = [(d, d + 4) for d in spot[3]] + [(d, d - 4) for d in spot[0]]
    pass_on = [(d, d + 4) for d in spot[0] + spot[1]] + [(d, d - 4) for d in spot[2] + spot[3]]
    outer_in = [(d, d ^ 1) for d in spot[0] + spot[3]]
    inner_out = [(d, d ^ 1) for d in spot[1] + spot[2]]
    chosen = [pltpu.SMEM((blocks + 1,), jnp.int32)]

    sent = jnp.broadcast_to(kv_lists.reshape(1, -1), (devices, levels * 2 * blocks))
    lists = lax.all_to_all(sent, "ctx", 0, 0, tiled=True)
    smem = (lists, kv_counts)
    own = jnp.concatenate([after(keys, sent), values], axis=0)
    other = permute(own, devices, other_core)
    far_rows = [2 * (blocks >> level) * rows for level, _ in shape["far"]]
    crossing, *far_packs = pack_call(first_pack, shape, lists, (own,), [row_count, *far_rows], chosen)
    crossed = permute(crossing, devices, over_y)
    far = []
    for (level, way), pack in zip(shape["far"], far_packs):
        step = (1 << level) * (1 - 2 * way)
        far.append(permute(pack, devices, [(d, d + step) for d in every]))
    rest_pack, along_pack = pack_call(
        second_pack, shape, lists, (own, other), [row_count // 2, row_count], chosen
    )
    state = attend_call(near_kernel, shape, smem, (queries, own, other))

    crossed, rest_pack, state, *far[:2] = lax.optimization_barrier((crossed, rest_pack, state, *far[:2]))
    passed = permute(crossed, devices, pass_on)
    rest = permute(rest_pack, devices, over_y)
    crossed_core = permute(crossed, devices, outer_in)
    along = permute(after(along_pack, *far), devices, outer_along)
    state = attend_call(quad_kernel, shape, smem, (queries, crossed, crossed_core, *far), state, False, chosen)

    along, rest, state = lax.optimization_barrier((along, rest, state))
    third = permute(along, devices, outer_swap)
    rest_core = permute(rest, devices, other_core)
    passed_core = permute(after(passed, rest_core), devices, inner_out)
    third_core = permute(after(third, passed_core), devices, outer_in)
    state = attend_call(passed_kernel, shape, smem, (queries, rest, rest_core, passed), state, False, chosen)
    return attend_call(last_kernel, shape, smem, (queries, passed_core, third, third_core), state, True, chosen)


def solution(mesh):
    in_specs = (
        P(("groups", "ctx"), None),
        P(("groups", "ctx"), None),
        P(("groups", "ctx"), None),
        P("ctx", None, None, None),
        P("ctx", None, None),
    )
    out_specs = P(("groups", "ctx"), None)
    return jax.shard_map(shards, mesh=mesh, in_specs=in_specs, out_specs=out_specs, check_vma=False)
```

```python
import functools
import math

import jax
import jax.numpy as jnp
from jax import lax
from jax.experimental import pallas as pl
from jax.experimental.pallas import tpu as pltpu
from jax.sharding import PartitionSpec as P

HEAD = 128
UNROLL = 20
MASKED = -1e30
F32 = jnp.float32
BF16 = jnp.bfloat16
VMEM = 8 * 1024 * 1024
COST = pl.CostEstimate(flops=1000, bytes_accessed=1000, transcendentals=0)


def permute(block, count, route):
    pairs = [(a, b) for a, b in route if 0 <= a < count and 0 <= b < count]
    return lax.ppermute(block, "ctx", pairs)


def listed(lists, device, level, side, j, shape):
    device = jnp.clip(device, 0, shape["devices"] - 1)
    return lists[device, (level * 2 + side) * shape["blocks"] + j]


def others(found, names, blocks):
    place = jnp.int32(0)
    for b in range(blocks):
        named = functools.reduce(jnp.logical_or, [n == b for n in names])
        found[place] = jnp.int32(b)
        place = place + jnp.where(named, 0, 1)


def gather(source, target, names, rows, at=0):
    below = source.shape[0] // 2
    for shift in (0, below):
        for name in names:
            target[at : at + rows] = source[pl.ds(pl.multiple_of(name * rows + shift, rows), rows)]
            at += rows
    return at


def far_pack(shape, lists, own, *far):
    me = lax.axis_index("ctx")
    for (level, way), out in zip(shape["far"], far):
        device = me + (1 << level) * (1 - 2 * way)
        names = [listed(lists, device, level, way, j, shape) for j in range(shape["blocks"] >> level)]
        gather(own, out, names, shape["rows"])


def crossing_names(found, lists, me, inner, shape):
    first = inner % 4 == 1
    half = shape["blocks"] // 2
    reader = jnp.where(first, inner - 2, inner + 2)
    names = [listed(lists, reader, 1, jnp.where(first, 1, 0), j, shape) for j in range(half)]
    others(found, names, shape["blocks"])
    return names, [found[j] for j in range(half)]


def reader_names(lists, me, shape):
    first = me % 4 < 2
    reader = me - me % 4 + jnp.where(first, 2, 1)
    return [listed(lists, reader, 1, jnp.where(first, 0, 1), j, shape) for j in range(shape["blocks"] // 2)]


def first_pack(shape, lists, own, crossing, *refs):
    far, found = refs[:-1], refs[-1]
    far_pack(shape, lists, own, *far)
    half = shape["blocks"] // 2
    me = lax.axis_index("ctx")
    spot = me % 4
    outer = jnp.logical_or(spot == 0, spot == 3)

    @pl.when(outer)
    def _():
        gather(own, crossing, reader_names(lists, me, shape), shape["rows"])

    @pl.when(jnp.logical_not(outer))
    def _():
        names, _ = crossing_names(found, lists, me, me, shape)
        gather(own, crossing, names, shape["rows"])


def second_pack(shape, lists, own, other, out, along, found):
    me = lax.axis_index("ctx")
    spot = me % 4
    outer = jnp.logical_or(spot == 0, spot == 3)
    quarter = shape["blocks"] // 4
    others(found, reader_names(lists, me, shape), shape["blocks"])
    late = [found[j] for j in range(2 * quarter)]

    @pl.when(outer)
    def _():
        gather(own, along, late[:quarter], shape["rows"])
        _, rest = crossing_names(found, lists, me, jnp.where(spot == 0, me + 1, me - 1), shape)
        gather(other, out, rest[quarter:], shape["rows"])

    @pl.when(jnp.logical_not(outer))
    def _():
        gather(other, along, late[quarter:], shape["rows"])
        _, rest = crossing_names(found, lists, me, me, shape)
        gather(own, out, rest[:quarter], shape["rows"])


SMEM = pl.BlockSpec(memory_space=pltpu.SMEM)
IN_VMEM = pl.BlockSpec(memory_space=pltpu.VMEM)


def pack_call(body, shape, lists, arrays, out_rows, scratch=()):
    width = arrays[0].shape[1]
    return pl.pallas_call(
        functools.partial(body, shape),
        out_shape=tuple(jax.ShapeDtypeStruct((r, width), BF16) for r in out_rows),
        in_specs=[SMEM] + [IN_VMEM] * len(arrays),
        out_specs=tuple([IN_VMEM] * len(out_rows)),
        scratch_shapes=list(scratch),
        cost_estimate=COST,
        compiler_params=pltpu.CompilerParams(vmem_limit_bytes=VMEM),
    )(lists, *arrays)


def lanes(column, n):
    wide = jnp.concatenate([column] * -(-n // column.shape[1]), axis=1)
    return wide[:, :n]


def attend(query, state, keys, values, masks):
    scale = math.log2(math.e) / math.sqrt(HEAD)
    raw = lax.dot_general(query, keys, (((1,), (1,)), ((), ())), preferred_element_type=F32)
    scores = []
    at = 0
    for n, mask in masks:
        part = raw[:, at : at + n] * scale
        scores.append(part if mask is None else part + mask)
        at += n
    scores = scores[0] if len(scores) == 1 else jnp.concatenate(scores, axis=1)
    best = jnp.broadcast_to(jnp.max(scores, axis=1, keepdims=True), query.shape)
    if state is not None:
        best = jnp.maximum(best, state[0])
    weights = jnp.exp2(scores - lanes(best, scores.shape[1])).astype(BF16)
    both = jnp.dot(weights, jnp.concatenate([values, jnp.ones_like(values)], axis=1), preferred_element_type=F32)
    weighted, total = both[:, :HEAD], both[:, HEAD:]
    if state is not None:
        factor = jnp.exp2(state[0] - best)
        total = total + state[1] * factor
        weighted = weighted + state[2] * factor
    return best, total, weighted


def member_flags(flags, at, ids, lists, counts, me, level, side, shape):
    counted = counts[0, level, side]
    names = [listed(lists, me, level, side, j, shape) for j in range(shape["blocks"] >> level)]
    for n, b in enumerate(ids):
        seen = functools.reduce(
            jnp.logical_or, [jnp.logical_and(j < counted, name == b) for j, name in enumerate(names)]
        )
        flags[at + n] = jnp.where(seen, 0.0, MASKED).astype(F32)


def order_flags(flags, at, capacity, counts, level, side):
    counted = counts[0, level, side]
    for j in range(capacity):
        flags[at + j] = jnp.where(j < counted, 0.0, MASKED).astype(F32)


def spread(flags, at, count, rows):
    place = lax.broadcasted_iota(jnp.int32, (1, count * rows), 1)
    row = jnp.full((1, count * rows), flags[at], F32)
    for b in range(1, count):
        row = jnp.where(place >= b * rows, flags[at + b], row)
    return row


def over_heads(width, body):
    def step(h, _):
        body(pl.ds(pl.multiple_of(h * HEAD, HEAD), HEAD))
        return 0

    lax.fori_loop(0, width // HEAD, step, 0, unroll=math.gcd(UNROLL, width // HEAD))


def load_state(refs, c):
    return tuple(ref[:, c] for ref in refs)


def store_state(refs, c, state):
    for ref, part in zip(refs, state):
        ref[:, c] = part


def far_sources(parts, refs, flags, at, counts, shape):
    sources = []
    for number, level, side in parts:
        capacity = shape["blocks"] >> level
        order_flags(flags, at, capacity, counts, level, side)
        sources.append((refs[number], 0, 2 * capacity * shape["rows"]))
        at += capacity
    return sources, at


def near_kernel(shape, lists, counts, q, own, other, *refs):
    after, flags = refs[-4:-1], refs[-1]
    me = lax.axis_index("ctx")
    blocks = shape["blocks"]
    member_flags(flags, 0, range(blocks), lists, counts, me, 0, 1 - me % 2, shape)
    mask = spread(flags, 0, blocks, shape["rows"])

    def head(c):
        keys, values = packed([own, other], c)
        masks = [(own.shape[0] // 2, None), (other.shape[0] // 2, mask)]
        store_state(after, c, attend(q[:, c], None, keys, values, masks))

    over_heads(shape["width"], head)


def packed(refs, c, filler=0):
    keys, values = [], []
    for ref in refs:
        ref, at, count = ref if isinstance(ref, tuple) else (ref, 0, ref.shape[0])
        keys.append(ref[at : at + count // 2, c])
        values.append(ref[at + count // 2 : at + count, c])
    if filler:
        keys.append(jnp.zeros((filler, HEAD), BF16))
        values.append(jnp.zeros((filler, HEAD), BF16))
    return jnp.concatenate(keys, axis=0), jnp.concatenate(values, axis=0)


def more_heads(shape, flags, count, q, before, after, sources):
    filler = -count % shape["blocks"]
    for b in range(count, count + filler):
        flags[b] = jnp.float32(MASKED)
    mask = spread(flags, 0, count + filler, shape["rows"])

    def head(c):
        keys, values = packed(sources, c, filler * shape["rows"])
        store_state(after, c, attend(q[:, c], load_state(before, c), keys, values, [(keys.shape[0], mask)]))

    over_heads(shape["width"], head)


def quad_kernel(shape, lists, counts, q, crossed, crossed_core, *refs):
    far, before, after, flags, found = refs[:-8], refs[-8:-5], refs[-5:-2], refs[-2], refs[-1]
    me = lax.axis_index("ctx")
    spot = me % 4
    blocks = shape["blocks"]
    half = blocks // 2
    begun = 0
    for level, way in shape["far"]:
        order_flags(flags, begun, blocks >> level, counts, level, way)
        begun += blocks >> level
    near_side = jnp.where(spot < 2, 1, 0)
    outer = jnp.logical_or(spot == 0, spot == 3)

    @pl.when(outer)
    def _():
        names, _ = crossing_names(found, lists, me, jnp.where(spot == 0, me + 2, me - 2), shape)
        member_flags(flags, begun, names, lists, counts, me, 1, near_side, shape)
        more_heads(shape, flags, begun + half, q, before, after, [*far, crossed])

    @pl.when(jnp.logical_not(outer))
    def _():
        order_flags(flags, begun, half, counts, 1, near_side)
        names, _ = crossing_names(found, lists, me, jnp.where(spot == 1, me + 1, me - 1), shape)
        member_flags(flags, begun + half, names, lists, counts, me, 0, me % 2, shape)
        more_heads(shape, flags, begun + 2 * half, q, before, after, [*far, crossed, crossed_core])


def giver_names(found, lists, me, shape):
    spot = me % 4
    outer = jnp.logical_or(spot == 0, spot == 3)
    step = jnp.where(outer, 3, 4)
    giver = jnp.where(spot < 2, me - step, me + step)
    half = shape["blocks"] // 2
    names = [listed(lists, giver, 1, jnp.where(spot < 2, 1, 0), j, shape) for j in range(half)]
    others(found, names, shape["blocks"])
    return names, [found[j] for j in range(half)]


def passed_kernel(shape, lists, counts, q, rest, rest_core, passed, *refs):
    before, after, flags, found = refs[:3], refs[3:6], refs[6], refs[7]
    me = lax.axis_index("ctx")
    spot = me % 4
    blocks = shape["blocks"]
    half = blocks // 2
    quarter = blocks // 4
    outer = jnp.logical_or(spot == 0, spot == 3)
    far_side = jnp.where(spot < 2, 0, 1)

    @pl.when(outer)
    def _():
        _, others_ = crossing_names(found, lists, me, jnp.where(spot == 0, me + 2, me - 2), shape)
        member_flags(flags, 0, others_, lists, counts, me, 1, jnp.where(spot < 2, 1, 0), shape)
        order_flags(flags, half, half, counts, 1, far_side)

    @pl.when(jnp.logical_not(outer))
    def _():
        _, others_ = crossing_names(found, lists, me, jnp.where(spot == 1, me + 1, me - 1), shape)
        member_flags(flags, 0, others_[quarter:] + others_[:quarter], lists, counts, me, 0, me % 2, shape)
        names, _ = giver_names(found, lists, me, shape)
        member_flags(flags, half, names, lists, counts, me, 1, far_side, shape)

    more_heads(shape, flags, 2 * half, q, before, after, [rest, rest_core, passed])


def last_kernel(shape, lists, counts, q, passed_core, third, third_core, *refs):
    before, out, flags, found = refs[:3], refs[3], refs[4], refs[5]
    me = lax.axis_index("ctx")
    spot = me % 4
    blocks = shape["blocks"]
    half = blocks // 2
    quarter = half // 2
    names, rest = giver_names(found, lists, me, shape)
    outer = jnp.logical_or(spot == 0, spot == 3)

    def heads(sources, count):
        filler = -count % blocks
        for b in range(count, count + filler):
            flags[b] = jnp.float32(MASKED)
        mask = spread(flags, 0, count + filler, shape["rows"])

        def head(c):
            keys, values = packed(sources, c, filler * shape["rows"])
            _, total, weighted = attend(q[:, c], load_state(before, c), keys, values, [(keys.shape[0], mask)])
            out[:, c] = (weighted / total).astype(BF16)

        over_heads(shape["width"], head)

    @pl.when(outer)
    def _():
        member_flags(flags, 0, names + rest[quarter:] + rest[:quarter], lists, counts, me, 0, me % 2, shape)
        heads([passed_core, third, third_core], 2 * half)

    @pl.when(jnp.logical_not(outer))
    def _():
        member_flags(flags, 0, rest, lists, counts, me, 1, jnp.where(spot < 2, 0, 1), shape)
        heads([third, third_core], half)


def attend_call(body, shape, smem, arrays, state=(), last=False, scratch=()):
    queries, width = arrays[0].shape
    return pl.pallas_call(
        functools.partial(body, shape),
        out_shape=jax.ShapeDtypeStruct((queries, width), BF16)
        if last
        else tuple([jax.ShapeDtypeStruct((queries, width), F32)] * 3),
        in_specs=[SMEM] * len(smem) + [IN_VMEM] * (len(arrays) + len(state)),
        out_specs=IN_VMEM if last else tuple([IN_VMEM] * 3),
        scratch_shapes=[pltpu.SMEM((64,), F32), *scratch],
        cost_estimate=COST,
        compiler_params=pltpu.CompilerParams(vmem_limit_bytes=VMEM),
    )(*smem, *arrays, *state)


def after(value, *events):
    return lax.optimization_barrier((value, *events))[0]


def shards(queries, keys, values, kv_lists, kv_counts):
    row_count, width = queries.shape
    blocks = kv_lists.shape[3]
    levels = kv_lists.shape[1]
    devices = lax.axis_size("ctx")
    half = blocks // 2
    rows = row_count // blocks
    shape = {"devices": devices, "blocks": blocks, "rows": rows, "width": width, "far": [(level, way) for level in range(2, levels) for way in range(2)]}
    every = range(devices)
    spot = {i: [d for d in every if d % 4 == i] for i in range(4)}
    other_core = [(d, d ^ 1) for d in every]
    over_y = [(d, d ^ 2) for d in every]
    outward = [(d, d + 4) for d in spot[2] + spot[3]] + [(d, d - 4) for d in spot[0] + spot[1]]
    pass_on = [(d, d + 4) for d in spot[0] + spot[1]] + [(d, d - 4) for d in spot[2] + spot[3]]
    outer_in = [(d, d ^ 1) for d in spot[0] + spot[3]]
    inner_out = [(d, d ^ 1) for d in spot[1] + spot[2]]
    chosen = [pltpu.SMEM((blocks + 1,), jnp.int32)]

    sent = jnp.broadcast_to(kv_lists.reshape(1, -1), (devices, levels * 2 * blocks))
    lists = lax.all_to_all(sent, "ctx", 0, 0, tiled=True)
    smem = (lists, kv_counts)
    own = jnp.concatenate([after(keys, sent), values], axis=0)
    other = permute(own, devices, other_core)
    far_rows = [2 * (blocks >> level) * rows for level, _ in shape["far"]]
    crossing, *far_packs = pack_call(first_pack, shape, lists, (own,), [row_count, *far_rows], chosen)
    crossed = permute(crossing, devices, over_y)
    far = []
    for (level, way), pack in zip(shape["far"], far_packs):
        step = (1 << level) * (1 - 2 * way)
        far.append(permute(pack, devices, [(d, d + step) for d in every]))
    rest_pack, along_pack = pack_call(
        second_pack, shape, lists, (own, other), [row_count // 2, row_count // 2], chosen
    )
    state = attend_call(near_kernel, shape, smem, (queries, own, other))

    crossed, rest_pack, along_pack, state, *far = lax.optimization_barrier(
        (crossed, rest_pack, along_pack, state, *far)
    )
    passed = permute(crossed, devices, pass_on)
    rest = permute(rest_pack, devices, over_y)
    crossed_core = permute(crossed, devices, outer_in)
    along = permute(along_pack, devices, outward)
    state = attend_call(quad_kernel, shape, smem, (queries, crossed, crossed_core, *far), state, False, chosen)

    along, rest, state = lax.optimization_barrier((along, rest, state))
    third = permute(along, devices, over_y)
    rest_core = permute(rest, devices, other_core)
    passed, rest_core, third = lax.optimization_barrier((passed, rest_core, third))
    passed_core = permute(passed, devices, inner_out)
    third_core = permute(third, devices, other_core)
    state = attend_call(passed_kernel, shape, smem, (queries, rest, rest_core, passed), state, False, chosen)
    return attend_call(last_kernel, shape, smem, (queries, passed_core, third, third_core), state, True, chosen)


def solution(mesh):
    in_specs = (
        P(("groups", "ctx"), None),
        P(("groups", "ctx"), None),
        P(("groups", "ctx"), None),
        P("ctx", None, None, None),
        P("ctx", None, None),
    )
    out_specs = P(("groups", "ctx"), None)
    return jax.shard_map(shards, mesh=mesh, in_specs=in_specs, out_specs=out_specs, check_vma=False)
```

```python
import functools
import math

import jax
import jax.numpy as jnp
from jax import lax
from jax.experimental import pallas as pl
from jax.experimental.pallas import tpu as pltpu
from jax.sharding import PartitionSpec as P

HEAD = 128
UNROLL = 20
MASKED = -1e30
F32 = jnp.float32
BF16 = jnp.bfloat16
VMEM = 8 * 1024 * 1024
COST = pl.CostEstimate(flops=1000, bytes_accessed=1000, transcendentals=0)


def permute(block, count, route):
    pairs = [(a, b) for a, b in route if 0 <= a < count and 0 <= b < count]
    return lax.ppermute(block, "ctx", pairs)


def listed(lists, device, level, side, j, shape):
    device = jnp.clip(device, 0, shape["devices"] - 1)
    return lists[device, (level * 2 + side) * shape["blocks"] + j]


def others(found, names, blocks):
    place = jnp.int32(0)
    for b in range(blocks):
        named = functools.reduce(jnp.logical_or, [n == b for n in names])
        found[place] = jnp.int32(b)
        place = place + jnp.where(named, 0, 1)


def gather(source, target, names, rows, at=0):
    below = source.shape[0] // 2
    for shift in (0, below):
        for name in names:
            target[at : at + rows] = source[pl.ds(pl.multiple_of(name * rows + shift, rows), rows)]
            at += rows
    return at


def far_pack(shape, lists, own, *far):
    me = lax.axis_index("ctx")
    for (level, way), out in zip(shape["far"], far):
        device = me + (1 << level) * (1 - 2 * way)
        names = [listed(lists, device, level, way, j, shape) for j in range(shape["blocks"] >> level)]
        gather(own, out, names, shape["rows"])


def crossing_names(found, lists, me, inner, shape):
    first = inner % 4 == 1
    half = shape["blocks"] // 2
    reader = jnp.where(first, inner - 2, inner + 2)
    names = [listed(lists, reader, 1, jnp.where(first, 1, 0), j, shape) for j in range(half)]
    others(found, names, shape["blocks"])
    return names, [found[j] for j in range(half)]


def reader_names(lists, me, shape):
    first = me % 4 < 2
    reader = me - me % 4 + jnp.where(first, 2, 1)
    return [listed(lists, reader, 1, jnp.where(first, 0, 1), j, shape) for j in range(shape["blocks"] // 2)]


def first_pack(shape, lists, own, crossing, *refs):
    far, found = refs[:-1], refs[-1]
    far_pack(shape, lists, own, *far)
    half = shape["blocks"] // 2
    me = lax.axis_index("ctx")
    spot = me % 4
    outer = jnp.logical_or(spot == 0, spot == 3)

    @pl.when(outer)
    def _():
        gather(own, crossing, reader_names(lists, me, shape), shape["rows"])

    @pl.when(jnp.logical_not(outer))
    def _():
        names, _ = crossing_names(found, lists, me, me, shape)
        gather(own, crossing, names, shape["rows"])


def second_pack(shape, lists, own, other, out, along, found):
    me = lax.axis_index("ctx")
    spot = me % 4
    outer = jnp.logical_or(spot == 0, spot == 3)
    quarter = shape["blocks"] // 4
    others(found, reader_names(lists, me, shape), shape["blocks"])
    late = [found[j] for j in range(2 * quarter)]

    @pl.when(outer)
    def _():
        gather(own, along, late[:quarter], shape["rows"])
        _, rest = crossing_names(found, lists, me, jnp.where(spot == 0, me + 1, me - 1), shape)
        gather(other, out, rest[quarter:], shape["rows"])

    @pl.when(jnp.logical_not(outer))
    def _():
        gather(other, along, late[quarter:], shape["rows"])
        _, rest = crossing_names(found, lists, me, me, shape)
        gather(own, out, rest[:quarter], shape["rows"])


SMEM = pl.BlockSpec(memory_space=pltpu.SMEM)
IN_VMEM = pl.BlockSpec(memory_space=pltpu.VMEM)


def pack_call(body, shape, lists, arrays, out_rows, scratch=()):
    width = arrays[0].shape[1]
    return pl.pallas_call(
        functools.partial(body, shape),
        out_shape=tuple(jax.ShapeDtypeStruct((r, width), BF16) for r in out_rows),
        in_specs=[SMEM] + [IN_VMEM] * len(arrays),
        out_specs=tuple([IN_VMEM] * len(out_rows)),
        scratch_shapes=list(scratch),
        cost_estimate=COST,
        compiler_params=pltpu.CompilerParams(vmem_limit_bytes=VMEM),
    )(lists, *arrays)


def lanes(column, n):
    wide = jnp.concatenate([column] * -(-n // column.shape[1]), axis=1)
    return wide[:, :n]


def attend(query, state, keys, values, masks):
    scale = math.log2(math.e) / math.sqrt(HEAD)
    raw = lax.dot_general(query, keys, (((1,), (1,)), ((), ())), preferred_element_type=F32)
    scores = []
    at = 0
    for n, mask in masks:
        part = raw[:, at : at + n] * scale
        scores.append(part if mask is None else part + mask)
        at += n
    scores = scores[0] if len(scores) == 1 else jnp.concatenate(scores, axis=1)
    best = jnp.broadcast_to(jnp.max(scores, axis=1, keepdims=True), query.shape)
    if state is not None:
        best = jnp.maximum(best, state[0])
    weights = jnp.exp2(scores - lanes(best, scores.shape[1])).astype(BF16)
    both = jnp.dot(weights, jnp.concatenate([values, jnp.ones_like(values)], axis=1), preferred_element_type=F32)
    weighted, total = both[:, :HEAD], both[:, HEAD:]
    if state is not None:
        factor = jnp.exp2(state[0] - best)
        total = total + state[1] * factor
        weighted = weighted + state[2] * factor
    return best, total, weighted


def member_flags(flags, at, ids, lists, counts, me, level, side, shape):
    counted = counts[0, level, side]
    names = [listed(lists, me, level, side, j, shape) for j in range(shape["blocks"] >> level)]
    for n, b in enumerate(ids):
        seen = functools.reduce(
            jnp.logical_or, [jnp.logical_and(j < counted, name == b) for j, name in enumerate(names)]
        )
        flags[at + n] = jnp.where(seen, 0.0, MASKED).astype(F32)


def order_flags(flags, at, capacity, counts, level, side):
    counted = counts[0, level, side]
    for j in range(capacity):
        flags[at + j] = jnp.where(j < counted, 0.0, MASKED).astype(F32)


def spread(flags, at, count, rows):
    place = lax.broadcasted_iota(jnp.int32, (1, count * rows), 1)
    row = jnp.full((1, count * rows), flags[at], F32)
    for b in range(1, count):
        row = jnp.where(place >= b * rows, flags[at + b], row)
    return row


def over_heads(width, body):
    def step(h, _):
        body(pl.ds(pl.multiple_of(h * HEAD, HEAD), HEAD))
        return 0

    lax.fori_loop(0, width // HEAD, step, 0, unroll=math.gcd(UNROLL, width // HEAD))


def load_state(refs, c):
    return tuple(ref[:, c] for ref in refs)


def store_state(refs, c, state):
    for ref, part in zip(refs, state):
        ref[:, c] = part


def far_sources(parts, refs, flags, at, counts, shape):
    sources = []
    for number, level, side in parts:
        capacity = shape["blocks"] >> level
        order_flags(flags, at, capacity, counts, level, side)
        sources.append((refs[number], 0, 2 * capacity * shape["rows"]))
        at += capacity
    return sources, at


def near_kernel(shape, lists, counts, q, own, other, *refs):
    after, flags = refs[-4:-1], refs[-1]
    me = lax.axis_index("ctx")
    blocks = shape["blocks"]
    member_flags(flags, 0, range(blocks), lists, counts, me, 0, 1 - me % 2, shape)
    mask = spread(flags, 0, blocks, shape["rows"])

    def head(c):
        keys, values = packed([own, other], c)
        masks = [(own.shape[0] // 2, None), (other.shape[0] // 2, mask)]
        store_state(after, c, attend(q[:, c], None, keys, values, masks))

    over_heads(shape["width"], head)


def packed(refs, c, filler=0):
    keys, values = [], []
    for ref in refs:
        ref, at, count = ref if isinstance(ref, tuple) else (ref, 0, ref.shape[0])
        keys.append(ref[at : at + count // 2, c])
        values.append(ref[at + count // 2 : at + count, c])
    if filler:
        keys.append(jnp.zeros((filler, HEAD), BF16))
        values.append(jnp.zeros((filler, HEAD), BF16))
    return jnp.concatenate(keys, axis=0), jnp.concatenate(values, axis=0)


def more_heads(shape, flags, count, q, before, after, sources):
    filler = -count % shape["blocks"]
    for b in range(count, count + filler):
        flags[b] = jnp.float32(MASKED)
    mask = spread(flags, 0, count + filler, shape["rows"])

    def head(c):
        keys, values = packed(sources, c, filler * shape["rows"])
        store_state(after, c, attend(q[:, c], load_state(before, c), keys, values, [(keys.shape[0], mask)]))

    over_heads(shape["width"], head)


def quad_kernel(shape, lists, counts, q, crossed, *refs):
    far, before, after, flags, found = refs[:-8], refs[-8:-5], refs[-5:-2], refs[-2], refs[-1]
    me = lax.axis_index("ctx")
    spot = me % 4
    blocks = shape["blocks"]
    half = blocks // 2
    begun = 0
    for level, way in shape["far"]:
        order_flags(flags, begun, blocks >> level, counts, level, way)
        begun += blocks >> level
    near_side = jnp.where(spot < 2, 1, 0)
    outer = jnp.logical_or(spot == 0, spot == 3)

    @pl.when(outer)
    def _():
        names, _ = crossing_names(found, lists, me, jnp.where(spot == 0, me + 2, me - 2), shape)
        member_flags(flags, begun, names, lists, counts, me, 1, near_side, shape)
        more_heads(shape, flags, begun + half, q, before, after, [*far, crossed])

    @pl.when(jnp.logical_not(outer))
    def _():
        order_flags(flags, begun, half, counts, 1, near_side)
        more_heads(shape, flags, begun + half, q, before, after, [*far, crossed])


def giver_names(found, lists, me, shape):
    spot = me % 4
    outer = jnp.logical_or(spot == 0, spot == 3)
    step = jnp.where(outer, 3, 4)
    giver = jnp.where(spot < 2, me - step, me + step)
    half = shape["blocks"] // 2
    names = [listed(lists, giver, 1, jnp.where(spot < 2, 1, 0), j, shape) for j in range(half)]
    others(found, names, shape["blocks"])
    return names, [found[j] for j in range(half)]


def rest_kernel(shape, lists, counts, q, rest, rest_core, *refs):
    before, after, flags, found = refs[:3], refs[3:6], refs[6], refs[7]
    me = lax.axis_index("ctx")
    spot = me % 4
    quarter = shape["blocks"] // 4
    outer = jnp.logical_or(spot == 0, spot == 3)

    @pl.when(outer)
    def _():
        _, ids = crossing_names(found, lists, me, jnp.where(spot == 0, me + 2, me - 2), shape)
        member_flags(flags, 0, ids, lists, counts, me, 1, jnp.where(spot < 2, 1, 0), shape)

    @pl.when(jnp.logical_not(outer))
    def _():
        _, ids = crossing_names(found, lists, me, jnp.where(spot == 1, me + 1, me - 1), shape)
        member_flags(flags, 0, ids[quarter:] + ids[:quarter], lists, counts, me, 0, me % 2, shape)

    more_heads(shape, flags, 2 * quarter, q, before, after, [rest, rest_core])


def passed_kernel(shape, lists, counts, q, crossed_core, passed, *refs):
    before, after, flags, found = refs[:3], refs[3:6], refs[6], refs[7]
    me = lax.axis_index("ctx")
    spot = me % 4
    half = shape["blocks"] // 2
    outer = jnp.logical_or(spot == 0, spot == 3)
    far_side = jnp.where(spot < 2, 0, 1)

    @pl.when(outer)
    def _():
        order_flags(flags, 0, half, counts, 1, far_side)
        more_heads(shape, flags, half, q, before, after, [passed])

    @pl.when(jnp.logical_not(outer))
    def _():
        names, _ = crossing_names(found, lists, me, jnp.where(spot == 1, me + 1, me - 1), shape)
        member_flags(flags, 0, names, lists, counts, me, 0, me % 2, shape)
        names, _ = giver_names(found, lists, me, shape)
        member_flags(flags, half, names, lists, counts, me, 1, far_side, shape)
        more_heads(shape, flags, 2 * half, q, before, after, [crossed_core, passed])


def last_kernel(shape, lists, counts, q, passed_core, third, third_core, *refs):
    before, out, flags, found = refs[:3], refs[3], refs[4], refs[5]
    me = lax.axis_index("ctx")
    spot = me % 4
    blocks = shape["blocks"]
    half = blocks // 2
    quarter = half // 2
    names, rest = giver_names(found, lists, me, shape)
    outer = jnp.logical_or(spot == 0, spot == 3)

    def heads(sources, count):
        filler = -count % blocks
        for b in range(count, count + filler):
            flags[b] = jnp.float32(MASKED)
        mask = spread(flags, 0, count + filler, shape["rows"])

        def head(c):
            keys, values = packed(sources, c, filler * shape["rows"])
            _, total, weighted = attend(q[:, c], load_state(before, c), keys, values, [(keys.shape[0], mask)])
            out[:, c] = (weighted / total).astype(BF16)

        over_heads(shape["width"], head)

    @pl.when(outer)
    def _():
        member_flags(flags, 0, names + rest[quarter:] + rest[:quarter], lists, counts, me, 0, me % 2, shape)
        heads([passed_core, third, third_core], 2 * half)

    @pl.when(jnp.logical_not(outer))
    def _():
        member_flags(flags, 0, rest, lists, counts, me, 1, jnp.where(spot < 2, 0, 1), shape)
        heads([third, third_core], half)


def attend_call(body, shape, smem, arrays, state=(), last=False, scratch=()):
    queries, width = arrays[0].shape
    return pl.pallas_call(
        functools.partial(body, shape),
        out_shape=jax.ShapeDtypeStruct((queries, width), BF16)
        if last
        else tuple([jax.ShapeDtypeStruct((queries, width), F32)] * 3),
        in_specs=[SMEM] * len(smem) + [IN_VMEM] * (len(arrays) + len(state)),
        out_specs=IN_VMEM if last else tuple([IN_VMEM] * 3),
        scratch_shapes=[pltpu.SMEM((64,), F32), *scratch],
        cost_estimate=COST,
        compiler_params=pltpu.CompilerParams(vmem_limit_bytes=VMEM),
    )(*smem, *arrays, *state)


def after(value, *events):
    return lax.optimization_barrier((value, *events))[0]


def shards(queries, keys, values, kv_lists, kv_counts):
    row_count, width = queries.shape
    blocks = kv_lists.shape[3]
    levels = kv_lists.shape[1]
    devices = lax.axis_size("ctx")
    half = blocks // 2
    rows = row_count // blocks
    shape = {"devices": devices, "blocks": blocks, "rows": rows, "width": width, "far": [(level, way) for level in range(2, levels) for way in range(2)]}
    every = range(devices)
    spot = {i: [d for d in every if d % 4 == i] for i in range(4)}
    other_core = [(d, d ^ 1) for d in every]
    over_y = [(d, d ^ 2) for d in every]
    outward = [(d, d + 4) for d in spot[2] + spot[3]] + [(d, d - 4) for d in spot[0] + spot[1]]
    pass_on = [(d, d + 4) for d in spot[0] + spot[1]] + [(d, d - 4) for d in spot[2] + spot[3]]
    outer_in = [(d, d ^ 1) for d in spot[0] + spot[3]]
    inner_out = [(d, d ^ 1) for d in spot[1] + spot[2]]
    chosen = [pltpu.SMEM((blocks + 1,), jnp.int32)]

    sent = jnp.broadcast_to(kv_lists.reshape(1, -1), (devices, levels * 2 * blocks))
    lists = lax.all_to_all(sent, "ctx", 0, 0, tiled=True)
    smem = (lists, kv_counts)
    own = jnp.concatenate([after(keys, sent), values], axis=0)
    other = permute(own, devices, other_core)
    far_rows = [2 * (blocks >> level) * rows for level, _ in shape["far"]]
    crossing, *far_packs = pack_call(first_pack, shape, lists, (own,), [row_count, *far_rows], chosen)
    crossed = permute(crossing, devices, over_y)
    far = []
    for (level, way), pack in zip(shape["far"], far_packs):
        step = (1 << level) * (1 - 2 * way)
        far.append(permute(pack, devices, [(d, d + step) for d in every]))
    rest_pack, along_pack = pack_call(
        second_pack, shape, lists, (own, other), [row_count // 2, row_count // 2], chosen
    )
    state = attend_call(near_kernel, shape, smem, (queries, own, other))

    crossed, rest_pack, along_pack, state, *far = lax.optimization_barrier(
        (crossed, rest_pack, along_pack, state, *far)
    )
    passed = permute(crossed, devices, pass_on)
    rest = permute(rest_pack, devices, over_y)
    along = permute(along_pack, devices, outward)
    state = attend_call(quad_kernel, shape, smem, (queries, crossed, *far), state, False, chosen)

    along, rest, crossed, state = lax.optimization_barrier((along, rest, crossed, state))
    third = permute(along, devices, over_y)
    rest_core = permute(rest, devices, other_core)
    crossed_core = permute(crossed, devices, outer_in)
    state = attend_call(rest_kernel, shape, smem, (queries, rest, rest_core), state, False, chosen)
    passed, third, state = lax.optimization_barrier((passed, third, state))
    passed_core = permute(passed, devices, inner_out)
    third, crossed_core = lax.optimization_barrier((third, crossed_core))
    third_core = permute(third, devices, other_core)
    state = attend_call(
        passed_kernel, shape, smem, (queries, crossed_core, passed), state, False, chosen
    )
    return attend_call(last_kernel, shape, smem, (queries, passed_core, third, third_core), state, True, chosen)


def solution(mesh):
    in_specs = (
        P(("groups", "ctx"), None),
        P(("groups", "ctx"), None),
        P(("groups", "ctx"), None),
        P("ctx", None, None, None),
        P("ctx", None, None),
    )
    out_specs = P(("groups", "ctx"), None)
    return jax.shard_map(shards, mesh=mesh, in_specs=in_specs, out_specs=out_specs, check_vma=False)
```

```python
import functools
import math

import jax
import jax.numpy as jnp
from jax import lax
from jax.experimental import pallas as pl
from jax.experimental.pallas import tpu as pltpu
from jax.sharding import PartitionSpec as P

HEAD = 128
UNROLL = 20
MASKED = -1e30
F32 = jnp.float32
BF16 = jnp.bfloat16
VMEM = 8 * 1024 * 1024
COST = pl.CostEstimate(flops=1000, bytes_accessed=1000, transcendentals=0)


def permute(block, count, route):
    pairs = [(a, b) for a, b in route if 0 <= a < count and 0 <= b < count]
    return lax.ppermute(block, "ctx", pairs)


def listed(lists, device, level, side, j, shape):
    device = jnp.clip(device, 0, shape["devices"] - 1)
    return lists[device, (level * 2 + side) * shape["blocks"] + j]


def others(found, names, blocks):
    place = jnp.int32(0)
    for b in range(blocks):
        named = functools.reduce(jnp.logical_or, [n == b for n in names])
        found[place] = jnp.int32(b)
        place = place + jnp.where(named, 0, 1)


def gather(source, target, names, rows, at=0):
    below = source.shape[0] // 2
    for shift in (0, below):
        for name in names:
            target[at : at + rows] = source[pl.ds(pl.multiple_of(name * rows + shift, rows), rows)]
            at += rows
    return at


def far_pack(shape, lists, own, *far):
    me = lax.axis_index("ctx")
    for (level, way), out in zip(shape["far"], far):
        device = me + (1 << level) * (1 - 2 * way)
        names = [listed(lists, device, level, way, j, shape) for j in range(shape["blocks"] >> level)]
        gather(own, out, names, shape["rows"])


def crossing_names(found, lists, me, inner, shape):
    first = inner % 4 == 1
    half = shape["blocks"] // 2
    reader = jnp.where(first, inner - 2, inner + 2)
    names = [listed(lists, reader, 1, jnp.where(first, 1, 0), j, shape) for j in range(half)]
    others(found, names, shape["blocks"])
    return names, [found[j] for j in range(half)]


def reader_names(lists, me, shape):
    first = me % 4 < 2
    reader = me - me % 4 + jnp.where(first, 2, 1)
    return [listed(lists, reader, 1, jnp.where(first, 0, 1), j, shape) for j in range(shape["blocks"] // 2)]


def first_pack(shape, lists, own, crossing, *refs):
    far, found = refs[:-1], refs[-1]
    far_pack(shape, lists, own, *far)
    half = shape["blocks"] // 2
    me = lax.axis_index("ctx")
    spot = me % 4
    outer = jnp.logical_or(spot == 0, spot == 3)

    @pl.when(outer)
    def _():
        gather(own, crossing, reader_names(lists, me, shape), shape["rows"])

    @pl.when(jnp.logical_not(outer))
    def _():
        names, _ = crossing_names(found, lists, me, me, shape)
        gather(own, crossing, names, shape["rows"])


def second_pack(shape, lists, own, other, out, along, found):
    me = lax.axis_index("ctx")
    spot = me % 4
    outer = jnp.logical_or(spot == 0, spot == 3)
    quarter = shape["blocks"] // 4
    others(found, reader_names(lists, me, shape), shape["blocks"])
    late = [found[j] for j in range(2 * quarter)]

    @pl.when(outer)
    def _():
        gather(own, along, late[:quarter], shape["rows"])
        _, rest = crossing_names(found, lists, me, jnp.where(spot == 0, me + 1, me - 1), shape)
        gather(other, out, rest[quarter:], shape["rows"])

    @pl.when(jnp.logical_not(outer))
    def _():
        gather(other, along, late[quarter:], shape["rows"])
        _, rest = crossing_names(found, lists, me, me, shape)
        gather(own, out, rest[:quarter], shape["rows"])


SMEM = pl.BlockSpec(memory_space=pltpu.SMEM)
IN_VMEM = pl.BlockSpec(memory_space=pltpu.VMEM)


def pack_call(body, shape, lists, arrays, out_rows, scratch=()):
    width = arrays[0].shape[1]
    return pl.pallas_call(
        functools.partial(body, shape),
        out_shape=tuple(jax.ShapeDtypeStruct((r, width), BF16) for r in out_rows),
        in_specs=[SMEM] + [IN_VMEM] * len(arrays),
        out_specs=tuple([IN_VMEM] * len(out_rows)),
        scratch_shapes=list(scratch),
        cost_estimate=COST,
        compiler_params=pltpu.CompilerParams(vmem_limit_bytes=VMEM),
    )(lists, *arrays)


def lanes(column, n):
    wide = jnp.concatenate([column] * -(-n // column.shape[1]), axis=1)
    return wide[:, :n]


def attend(query, state, keys, values, masks):
    scale = math.log2(math.e) / math.sqrt(HEAD)
    raw = lax.dot_general(query, keys, (((1,), (1,)), ((), ())), preferred_element_type=F32)
    scores = []
    at = 0
    for n, mask in masks:
        part = raw[:, at : at + n] * scale
        scores.append(part if mask is None else part + mask)
        at += n
    scores = scores[0] if len(scores) == 1 else jnp.concatenate(scores, axis=1)
    best = jnp.broadcast_to(jnp.max(scores, axis=1, keepdims=True), query.shape)
    if state is not None:
        best = jnp.maximum(best, state[0])
    weights = jnp.exp2(scores - lanes(best, scores.shape[1])).astype(BF16)
    both = jnp.dot(weights, jnp.concatenate([values, jnp.ones_like(values)], axis=1), preferred_element_type=F32)
    weighted, total = both[:, :HEAD], both[:, HEAD:]
    if state is not None:
        factor = jnp.exp2(state[0] - best)
        total = total + state[1] * factor
        weighted = weighted + state[2] * factor
    return best, total, weighted


def member_flags(flags, at, ids, lists, counts, me, level, side, shape):
    counted = counts[0, level, side]
    names = [listed(lists, me, level, side, j, shape) for j in range(shape["blocks"] >> level)]
    for n, b in enumerate(ids):
        seen = functools.reduce(
            jnp.logical_or, [jnp.logical_and(j < counted, name == b) for j, name in enumerate(names)]
        )
        flags[at + n] = jnp.where(seen, 0.0, MASKED).astype(F32)


def order_flags(flags, at, capacity, counts, level, side):
    counted = counts[0, level, side]
    for j in range(capacity):
        flags[at + j] = jnp.where(j < counted, 0.0, MASKED).astype(F32)


def spread(flags, at, count, rows):
    place = lax.broadcasted_iota(jnp.int32, (1, count * rows), 1)
    row = jnp.full((1, count * rows), flags[at], F32)
    for b in range(1, count):
        row = jnp.where(place >= b * rows, flags[at + b], row)
    return row


def over_heads(width, body):
    def step(h, _):
        body(pl.ds(pl.multiple_of(h * HEAD, HEAD), HEAD))
        return 0

    lax.fori_loop(0, width // HEAD, step, 0, unroll=math.gcd(UNROLL, width // HEAD))


def load_state(refs, c):
    return tuple(ref[:, c] for ref in refs)


def store_state(refs, c, state):
    for ref, part in zip(refs, state):
        ref[:, c] = part


def far_sources(parts, refs, flags, at, counts, shape):
    sources = []
    for number, level, side in parts:
        capacity = shape["blocks"] >> level
        order_flags(flags, at, capacity, counts, level, side)
        sources.append((refs[number], 0, 2 * capacity * shape["rows"]))
        at += capacity
    return sources, at


def near_kernel(shape, lists, counts, q, own, other, *refs):
    after, flags = refs[-4:-1], refs[-1]
    me = lax.axis_index("ctx")
    blocks = shape["blocks"]
    member_flags(flags, 0, range(blocks), lists, counts, me, 0, 1 - me % 2, shape)
    mask = spread(flags, 0, blocks, shape["rows"])

    def head(c):
        keys, values = packed([own, other], c)
        masks = [(own.shape[0] // 2, None), (other.shape[0] // 2, mask)]
        store_state(after, c, attend(q[:, c], None, keys, values, masks))

    over_heads(shape["width"], head)


def packed(refs, c, filler=0):
    keys, values = [], []
    for ref in refs:
        ref, at, count = ref if isinstance(ref, tuple) else (ref, 0, ref.shape[0])
        keys.append(ref[at : at + count // 2, c])
        values.append(ref[at + count // 2 : at + count, c])
    if filler:
        keys.append(jnp.zeros((filler, HEAD), BF16))
        values.append(jnp.zeros((filler, HEAD), BF16))
    return jnp.concatenate(keys, axis=0), jnp.concatenate(values, axis=0)


def more_heads(shape, flags, count, q, before, after, sources):
    filler = -count % shape["blocks"]
    for b in range(count, count + filler):
        flags[b] = jnp.float32(MASKED)
    mask = spread(flags, 0, count + filler, shape["rows"])

    def head(c):
        keys, values = packed(sources, c, filler * shape["rows"])
        store_state(after, c, attend(q[:, c], load_state(before, c), keys, values, [(keys.shape[0], mask)]))

    over_heads(shape["width"], head)


def quad_kernel(shape, lists, counts, q, crossed, *refs):
    far, before, after, flags, found = refs[:-8], refs[-8:-5], refs[-5:-2], refs[-2], refs[-1]
    me = lax.axis_index("ctx")
    spot = me % 4
    blocks = shape["blocks"]
    half = blocks // 2
    begun = 0
    for level, way in shape["far"]:
        order_flags(flags, begun, blocks >> level, counts, level, way)
        begun += blocks >> level
    near_side = jnp.where(spot < 2, 1, 0)
    outer = jnp.logical_or(spot == 0, spot == 3)

    @pl.when(outer)
    def _():
        names, _ = crossing_names(found, lists, me, jnp.where(spot == 0, me + 2, me - 2), shape)
        member_flags(flags, begun, names, lists, counts, me, 1, near_side, shape)
        more_heads(shape, flags, begun + half, q, before, after, [*far, crossed])

    @pl.when(jnp.logical_not(outer))
    def _():
        order_flags(flags, begun, half, counts, 1, near_side)
        more_heads(shape, flags, begun + half, q, before, after, [*far, crossed])


def giver_names(found, lists, me, shape):
    spot = me % 4
    outer = jnp.logical_or(spot == 0, spot == 3)
    step = jnp.where(outer, 3, 4)
    giver = jnp.where(spot < 2, me - step, me + step)
    half = shape["blocks"] // 2
    names = [listed(lists, giver, 1, jnp.where(spot < 2, 1, 0), j, shape) for j in range(half)]
    others(found, names, shape["blocks"])
    return names, [found[j] for j in range(half)]


def rest_kernel(shape, lists, counts, q, rest, rest_core, *refs):
    before, after, flags, found = refs[:3], refs[3:6], refs[6], refs[7]
    me = lax.axis_index("ctx")
    spot = me % 4
    quarter = shape["blocks"] // 4
    outer = jnp.logical_or(spot == 0, spot == 3)

    @pl.when(outer)
    def _():
        _, ids = crossing_names(found, lists, me, jnp.where(spot == 0, me + 2, me - 2), shape)
        member_flags(flags, 0, ids, lists, counts, me, 1, jnp.where(spot < 2, 1, 0), shape)

    @pl.when(jnp.logical_not(outer))
    def _():
        _, ids = crossing_names(found, lists, me, jnp.where(spot == 1, me + 1, me - 1), shape)
        member_flags(flags, 0, ids[quarter:] + ids[:quarter], lists, counts, me, 0, me % 2, shape)

    more_heads(shape, flags, 2 * quarter, q, before, after, [rest, rest_core])


def passed_kernel(shape, lists, counts, q, passed, *refs):
    before, after, flags, found = refs[:3], refs[3:6], refs[6], refs[7]
    me = lax.axis_index("ctx")
    spot = me % 4
    half = shape["blocks"] // 2
    outer = jnp.logical_or(spot == 0, spot == 3)
    far_side = jnp.where(spot < 2, 0, 1)

    @pl.when(outer)
    def _():
        order_flags(flags, 0, half, counts, 1, far_side)

    @pl.when(jnp.logical_not(outer))
    def _():
        names, _ = giver_names(found, lists, me, shape)
        member_flags(flags, 0, names, lists, counts, me, 1, far_side, shape)

    more_heads(shape, flags, half, q, before, after, [passed])


def last_kernel(shape, lists, counts, q, passed_core, crossed_core, third, third_core, *refs):
    before, out, flags, found = refs[:3], refs[3], refs[4], refs[5]
    me = lax.axis_index("ctx")
    spot = me % 4
    blocks = shape["blocks"]
    half = blocks // 2
    quarter = half // 2
    names, rest = giver_names(found, lists, me, shape)
    outer = jnp.logical_or(spot == 0, spot == 3)

    @pl.when(outer)
    def _():
        member_flags(flags, 0, names + rest[quarter:] + rest[:quarter], lists, counts, me, 0, me % 2, shape)

    @pl.when(jnp.logical_not(outer))
    def _():
        member_flags(flags, half, rest, lists, counts, me, 1, jnp.where(spot < 2, 0, 1), shape)
        crossed, _ = crossing_names(found, lists, me, jnp.where(spot == 1, me + 1, me - 1), shape)
        member_flags(flags, 0, crossed, lists, counts, me, 0, me % 2, shape)

    mask = spread(flags, 0, blocks, shape["rows"])

    def head(c):
        outer_parts = packed([passed_core], c)
        inner_parts = packed([crossed_core], c)
        later = packed([third, third_core], c)
        keys, values = [
            jnp.concatenate([jnp.where(outer, x, y), z], axis=0) for x, y, z in zip(outer_parts, inner_parts, later)
        ]
        _, total, weighted = attend(q[:, c], load_state(before, c), keys, values, [(keys.shape[0], mask)])
        out[:, c] = (weighted / total).astype(BF16)

    over_heads(shape["width"], head)


def attend_call(body, shape, smem, arrays, state=(), last=False, scratch=()):
    queries, width = arrays[0].shape
    return pl.pallas_call(
        functools.partial(body, shape),
        out_shape=jax.ShapeDtypeStruct((queries, width), BF16)
        if last
        else tuple([jax.ShapeDtypeStruct((queries, width), F32)] * 3),
        in_specs=[SMEM] * len(smem) + [IN_VMEM] * (len(arrays) + len(state)),
        out_specs=IN_VMEM if last else tuple([IN_VMEM] * 3),
        scratch_shapes=[pltpu.SMEM((64,), F32), *scratch],
        cost_estimate=COST,
        compiler_params=pltpu.CompilerParams(vmem_limit_bytes=VMEM),
    )(*smem, *arrays, *state)


def after(value, *events):
    return lax.optimization_barrier((value, *events))[0]


def shards(queries, keys, values, kv_lists, kv_counts):
    row_count, width = queries.shape
    blocks = kv_lists.shape[3]
    levels = kv_lists.shape[1]
    devices = lax.axis_size("ctx")
    half = blocks // 2
    rows = row_count // blocks
    shape = {"devices": devices, "blocks": blocks, "rows": rows, "width": width, "far": [(level, way) for level in range(2, levels) for way in range(2)]}
    every = range(devices)
    spot = {i: [d for d in every if d % 4 == i] for i in range(4)}
    other_core = [(d, d ^ 1) for d in every]
    over_y = [(d, d ^ 2) for d in every]
    outward = [(d, d + 4) for d in spot[2] + spot[3]] + [(d, d - 4) for d in spot[0] + spot[1]]
    pass_on = [(d, d + 4) for d in spot[0] + spot[1]] + [(d, d - 4) for d in spot[2] + spot[3]]
    outer_in = [(d, d ^ 1) for d in spot[0] + spot[3]]
    inner_out = [(d, d ^ 1) for d in spot[1] + spot[2]]
    chosen = [pltpu.SMEM((blocks + 1,), jnp.int32)]

    sent = jnp.broadcast_to(kv_lists.reshape(1, -1), (devices, levels * 2 * blocks))
    lists = lax.all_to_all(sent, "ctx", 0, 0, tiled=True)
    smem = (lists, kv_counts)
    own = jnp.concatenate([after(keys, sent), values], axis=0)
    other = permute(own, devices, other_core)
    far_rows = [2 * (blocks >> level) * rows for level, _ in shape["far"]]
    crossing, *far_packs = pack_call(first_pack, shape, lists, (own,), [row_count, *far_rows], chosen)
    crossed = permute(crossing, devices, over_y)
    far = []
    for (level, way), pack in zip(shape["far"], far_packs):
        step = (1 << level) * (1 - 2 * way)
        far.append(permute(pack, devices, [(d, d + step) for d in every]))
    rest_pack, along_pack = pack_call(
        second_pack, shape, lists, (own, other), [row_count // 2, row_count // 2], chosen
    )
    state = attend_call(near_kernel, shape, smem, (queries, own, other))

    crossed, rest_pack, along_pack, state, *far = lax.optimization_barrier(
        (crossed, rest_pack, along_pack, state, *far)
    )
    passed = permute(crossed, devices, pass_on)
    rest = permute(rest_pack, devices, over_y)
    along = permute(along_pack, devices, outward)
    state = attend_call(quad_kernel, shape, smem, (queries, crossed, *far), state, False, chosen)

    along, rest, crossed, state = lax.optimization_barrier((along, rest, crossed, state))
    third = permute(along, devices, over_y)
    rest_core = permute(rest, devices, other_core)
    crossed_core = permute(crossed, devices, outer_in)
    state = attend_call(rest_kernel, shape, smem, (queries, rest, rest_core), state, False, chosen)
    passed, third, state = lax.optimization_barrier((passed, third, state))
    passed_core = permute(passed, devices, inner_out)
    third, crossed_core = lax.optimization_barrier((third, crossed_core))
    third_core = permute(third, devices, other_core)
    state = attend_call(
        passed_kernel, shape, smem, (queries, passed), state, False, chosen
    )
    return attend_call(last_kernel, shape, smem, (queries, passed_core, crossed_core, third, third_core), state, True, chosen)


def solution(mesh):
    in_specs = (
        P(("groups", "ctx"), None),
        P(("groups", "ctx"), None),
        P(("groups", "ctx"), None),
        P("ctx", None, None, None),
        P("ctx", None, None),
    )
    out_specs = P(("groups", "ctx"), None)
    return jax.shard_map(shards, mesh=mesh, in_specs=in_specs, out_specs=out_specs, check_vma=False)
```
